32 devices in a mesh: wide: 8 (over y, x, core), narrow: 4 (over z).
Axes of the slice: x: 2, y: 2, z: 4, core: 2. Of those that a mesh axis runs over, the one named last changes fastest.
Arguments:
- wavefunction: float32 [2, 512, 512, 256], P(None, 'wide', 'narrow'), may hold values from -6 to 6
- previous_slope: float32 [2, 512, 512, 256], P(None, 'wide', 'narrow'), may hold values from -6 to 6
- potential: float32 [512, 512, 256], P('wide', 'narrow'), may hold values from 0.5 to 3
- kinetic_one: float32 [512, 512], replicated, as said below
- coupling_one: float32 [512, 512], replicated, as said below
- kinetic_two: float32 [512, 512], P('narrow'), as said below
- coupling_two: float32 [512, 512], P('narrow'), as said below
- kinetic_three: float32 [256, 256], replicated, as said below
- coupling_three: float32 [256, 256], replicated, as said below
Outputs:
- slope: float32 [2, 512, 512, 256], P(None, 'wide', 'narrow')
- next_input: float32 [2, 512, 512, 256], P(None, 'wide', 'narrow')
The draws below stay inside these ranges and needn't reach their ends.
Inputs may be any that keep to these rules, and one draw needn't show every extreme that they name: kinetic_one is symmetric. coupling_one is symmetric. kinetic_two is symmetric. coupling_two is symmetric. kinetic_three is symmetric. coupling_three is symmetric.
All inputs are finite; a program needn't handle non-finite values.
Results may differ from the reference program's by a relative error of at most 0.00005.
Values sent between devices are 32-bit elements; how exact they have to be, the bound alone decides.
A program may use at most 384 MiB of HBM per device.

```python
import jax
import jax.numpy as jnp
from jax import lax

N1 = 512
N2 = 512
N3 = 256


def symmetric_matrix(key, order):
    values = jax.random.normal(key, (order, order), jnp.float32)
    return (values + values.T) * (1.0 / jnp.sqrt(2.0 * order))


def draw_kinetic_one(key, part):
    return symmetric_matrix(jax.random.fold_in(key, 11), N1)


def draw_coupling_one(key, part):
    return symmetric_matrix(jax.random.fold_in(key, 12), N1)


def draw_kinetic_two(key, part):
    return symmetric_matrix(jax.random.fold_in(key, 13), N2)


def draw_coupling_two(key, part):
    return symmetric_matrix(jax.random.fold_in(key, 14), N2)


def draw_kinetic_three(key, part):
    return symmetric_matrix(jax.random.fold_in(key, 15), N3)


def draw_coupling_three(key, part):
    return symmetric_matrix(jax.random.fold_in(key, 16), N3)


def steps_of(key, dims, split, least, largest):
    level = 1.0
    for position, shards_of in split:
        steps = jax.random.uniform(jax.random.fold_in(jax.random.fold_in(key, 6), position), (shards_of,), jnp.float32, least / len(split), largest / len(split))
        level = level * jnp.repeat(jnp.exp(steps), dims[position] // shards_of).reshape((-1,) + (1,) * (len(dims) - 1 - position))
    return level


def bell_draw(key, dims, width, limit, cuts=(), held_as=jnp.bfloat16):
    level = steps_of(key, dims, cuts, -0.22, 0.18) if cuts else 1.0
    result = jax.random.normal(key, dims, jnp.float32) * width * level
    return jnp.minimum(jnp.maximum(result, -limit), limit).astype(held_as)


def setup_inputs(seed: int = 0) -> dict:
    seeds = jax.random.split(jax.random.key(seed), 10)
    wavefunction = bell_draw(seeds[0], (2, N1, N2, N3), 1.0, 6.0, ((1, 8), (2, 4)), jnp.float32)
    previous_slope = bell_draw(seeds[1], (2, N1, N2, N3), 1.0, 6.0, ((1, 8), (2, 4)), jnp.float32)
    potential = jnp.clip(0.5 + 2.5 * jax.random.uniform(seeds[2], (N1, N2, N3), jnp.float32) ** steps_of(seeds[2], (N1, N2, N3), ((0, 8), (1, 4)), -0.2, 0.2), 0.5, 3.0)
    kinetic_one = draw_kinetic_one(jax.random.fold_in(seeds[9], 71), 0)
    coupling_one = draw_coupling_one(jax.random.fold_in(seeds[9], 71), 0)
    kinetic_two = draw_kinetic_two(jax.random.fold_in(seeds[9], 71), 0)
    coupling_two = draw_coupling_two(jax.random.fold_in(seeds[9], 71), 0)
    kinetic_three = draw_kinetic_three(jax.random.fold_in(seeds[9], 71), 0)
    coupling_three = draw_coupling_three(jax.random.fold_in(seeds[9], 71), 0)
    return dict(wavefunction=wavefunction, previous_slope=previous_slope, potential=potential, kinetic_one=kinetic_one, coupling_one=coupling_one, kinetic_two=kinetic_two, coupling_two=coupling_two, kinetic_three=kinetic_three, coupling_three=coupling_three)


half_step = 0.1


def along_one(matrix, field):
    return jnp.einsum("ij,cjkl->cikl", matrix, field, precision=lax.Precision.HIGHEST)


def along_two(matrix, field):
    return jnp.einsum("ij,ckjl->ckil", matrix, field, precision=lax.Precision.HIGHEST)


def along_three(matrix, field):
    return jnp.einsum("ij,cklj->ckli", matrix, field, precision=lax.Precision.HIGHEST)


def reference(wavefunction, previous_slope, potential, kinetic_one, coupling_one, kinetic_two, coupling_two, kinetic_three, coupling_three):
    section_in = wavefunction + half_step * previous_slope
    hamil = along_one(kinetic_one, section_in)
    hamil = hamil + along_two(kinetic_two, section_in)
    hamil = hamil + along_three(kinetic_three, section_in)
    coupled = along_one(coupling_one, along_two(coupling_two, along_three(coupling_three, section_in)))
    hamil = hamil + coupled + potential[None] * section_in
    slope = jnp.stack([hamil[1], -hamil[0]])
    next_input = wavefunction + half_step * slope
    return (slope, next_input)
```

```python
import jax
import jax.numpy as jnp
from jax import lax
from jax.sharding import PartitionSpec as P

half_step = 0.1
HIGH = lax.Precision.HIGH


def along_one(matrix, field):
    return jnp.einsum("ij,jkl->ikl", matrix, field, precision=HIGH)


def along_two(matrix, field):
    return jnp.einsum("ij,kjl->kil", matrix, field, precision=HIGH)


def along_three(matrix, field):
    return jnp.einsum("ij,klj->kli", matrix, field, precision=HIGH)


def to_whole_one(field, wide):
    rows, second, third = field.shape
    blocks = field.reshape(rows, wide, second // wide, third).transpose(1, 0, 2, 3)
    moved = lax.all_to_all(blocks, "wide", split_axis=0, concat_axis=0, tiled=True)
    return moved.reshape(wide * rows, second // wide, third)


def from_whole_one(field, wide):
    rows, second, third = field.shape
    blocks = field.reshape(wide, rows // wide, second, third)
    moved = lax.all_to_all(blocks, "wide", split_axis=0, concat_axis=0, tiled=True)
    return moved.transpose(1, 0, 2, 3).reshape(rows // wide, wide * second, third)


def local(
    wide,
    wavefunction,
    previous_slope,
    potential,
    kinetic_one,
    coupling_one,
    kinetic_two,
    coupling_two,
    kinetic_three,
    coupling_three,
):
    sections = [wavefunction[c] + half_step * previous_slope[c] for c in range(2)]
    gathered = [lax.all_gather(s, "narrow", axis=1, tiled=True) for s in sections]
    whole = [to_whole_one(s, wide) for s in sections]
    base = [along_three(kinetic_three, s) + potential * s for s in sections]
    kinetic = [along_one(kinetic_one, s) for s in whole]
    hamil = []
    for c in range(2):
        coupled = along_three(coupling_three, along_two(coupling_two, gathered[c]))
        summed = kinetic[c] + along_one(coupling_one, to_whole_one(coupled, wide))
        hamil.append(from_whole_one(summed, wide) + along_two(kinetic_two, gathered[c]) + base[c])
    slope = jnp.stack([hamil[1], -hamil[0]])
    next_input = wavefunction + half_step * slope
    return (slope, next_input)


def solution(mesh):
    wide = mesh.shape["wide"]
    in_specs = (
        P(None, "wide", "narrow", None),
        P(None, "wide", "narrow", None),
        P("wide", "narrow", None),
        P(),
        P(),
        P("narrow", None),
        P("narrow", None),
        P(),
        P(),
    )
    out_specs = (P(None, "wide", "narrow", None), P(None, "wide", "narrow", None))

    def body(*arrays):
        return local(wide, *arrays)

    return jax.shard_map(body, mesh=mesh, in_specs=in_specs, out_specs=out_specs, check_vma=False)
```

```python
import jax
import jax.numpy as jnp
from jax import lax
from jax.sharding import PartitionSpec as P

half_step = 0.1
pieces = 2
HIGH = lax.Precision.HIGH


def along_one(matrix, field):
    return jnp.einsum("ij,jkl->ikl", matrix, field, precision=HIGH)


def along_two(matrix, field):
    return jnp.einsum("ij,kjl->kil", matrix, field, precision=HIGH)


def along_three(matrix, field):
    return jnp.einsum("ij,klj->kli", matrix, field, precision=HIGH)


def to_whole_one(field, wide):
    rows, second, third = field.shape
    blocks = field.reshape(rows, wide, second // wide, third).transpose(1, 0, 2, 3)
    moved = lax.all_to_all(blocks, "wide", split_axis=0, concat_axis=0, tiled=True)
    return moved.reshape(wide * rows, second // wide, third)


def from_whole_one(field, wide):
    rows, second, third = field.shape
    blocks = field.reshape(wide, rows // wide, second, third)
    moved = lax.all_to_all(blocks, "wide", split_axis=0, concat_axis=0, tiled=True)
    return moved.transpose(1, 0, 2, 3).reshape(rows // wide, wide * second, third)


def two_weights(kinetic_two, coupling_two):
    me = lax.axis_index("narrow")
    size = kinetic_two.shape[0]
    hub = jnp.where((me == 1) | (me == 2), 1.0, 0.0)
    slots = (me, jnp.maximum(me - 1, 0), jnp.minimum(me + 1, 3), jnp.where(me == 1, 3, 0))
    result = []
    for matrix in (coupling_two, kinetic_two):
        ends = lax.ppermute(matrix, "narrow", [(0, 1), (3, 2)])
        for rows in (ends, matrix * hub):
            result.append(jnp.concatenate([lax.dynamic_slice_in_dim(rows, slot * size, size, 1) for slot in slots], axis=1))
    return result


def middle_terms(weights, section):
    me = lax.axis_index("narrow")
    lower = lax.ppermute(section, "narrow", [(0, 1), (1, 2)])
    upper = lax.ppermute(section, "narrow", [(3, 2), (2, 1)])
    far = lax.ppermute(jnp.where(me == 1, lower, upper), "narrow", [(1, 2), (2, 1)])
    field = jnp.concatenate([section, lower, upper, far], axis=1)
    coupling_ends, coupling_own, kinetic_ends, kinetic_own = weights
    result = []
    for ends, own in ((coupling_ends, coupling_own), (kinetic_ends, kinetic_own)):
        received = lax.ppermute(along_two(ends, field), "narrow", [(1, 0), (2, 3)])
        result.append(along_two(own, field) + received)
    return result


def local(
    wide,
    wavefunction,
    previous_slope,
    potential,
    kinetic_one,
    coupling_one,
    kinetic_two,
    coupling_two,
    kinetic_three,
    coupling_three,
):
    rows = wavefunction.shape[1]
    half = rows // pieces
    sections = [wavefunction[c] + half_step * previous_slope[c] for c in range(2)]
    weights = two_weights(kinetic_two, coupling_two)
    second = [[middle_terms(weights, s[p * half:(p + 1) * half]) for p in range(pieces)] for s in sections]
    whole = [to_whole_one(s, wide) for s in sections]
    kinetic = [along_one(kinetic_one, s) for s in whole]
    base = [along_three(kinetic_three, s) + potential * s for s in sections]
    hamil = []
    for c in range(2):
        coupled = jnp.concatenate([along_three(coupling_three, terms[0]) for terms in second[c]])
        summed = kinetic[c] + along_one(coupling_one, to_whole_one(coupled, wide))
        middle = jnp.concatenate([terms[1] for terms in second[c]])
        hamil.append(from_whole_one(summed, wide) + middle + base[c])
    slope = jnp.stack([hamil[1], -hamil[0]])
    next_input = wavefunction + half_step * slope
    return (slope, next_input)


def solution(mesh):
    wide = mesh.shape["wide"]
    in_specs = (
        P(None, "wide", "narrow", None),
        P(None, "wide", "narrow", None),
        P("wide", "narrow", None),
        P(),
        P(),
        P("narrow", None),
        P("narrow", None),
        P(),
        P(),
    )
    out_specs = (P(None, "wide", "narrow", None), P(None, "wide", "narrow", None))

    def body(*arrays):
        return local(wide, *arrays)

    return jax.shard_map(body, mesh=mesh, in_specs=in_specs, out_specs=out_specs, check_vma=False)
```
